32 devices in a mesh: groups: 2 (over x), dom: 16 (over z, y, core).
Axes of the slice: x: 2, y: 2, z: 4, core: 2. Of those that a mesh axis runs over, the one named last changes fastest.
Arguments:
- node_feats: bfloat16 [32768, 256], P(('groups', 'dom')), parts along dimension 0, may hold values from -6 to 6
- tile_vals: bfloat16 [256, 24, 128, 128], P(('groups', 'dom')), parts along dimension 0, may hold values from 0 to 16, as said below
- tile_cols: int32 [256, 24], P(('groups', 'dom')), parts along dimension 0, may hold values from 0 to 127, as said below
- tile_count: int32 [256], P(('groups', 'dom')), parts along dimension 0, may hold values from 1 to 24, 1536 in all
- hist_cache: bfloat16 [2048, 256], P(('groups', 'dom')), parts along dimension 0, may hold values from -6 to 6
- bound_ids: int32 [256, 128], P(('groups', 'dom')), parts along dimension 0, may hold values from 0 to 1023, as said below
- bound_wts: bfloat16 [32768, 128], P(('groups', 'dom')), parts along dimension 0, may hold values from 0.049804688 to 1
- w_self: bfloat16 [256, 256], replicated, may hold values from -0.375 to 0.375
- w_neigh: bfloat16 [256, 256], replicated, may hold values from -6 to 6
- out_bias: float32 [256], replicated, may hold values from -3 to 3
- out_grad: bfloat16 [32768, 256], P(('groups', 'dom')), parts along dimension 0, may hold values from -6 to 6
Outputs:
- hidden_out: bfloat16 [32768, 256], P(('groups', 'dom')), parts along dimension 0
- feat_grad: bfloat16 [32768, 256], P(('groups', 'dom')), parts along dimension 0
- self_grad: float32 [512, 256], P('groups'), parts along dimension 0
- neigh_grad: float32 [512, 256], P('groups'), parts along dimension 0
- bias_grad: float32 [512], P('groups'), parts along dimension 0
The draws below stay inside these ranges and needn't reach their ends.
There are 2 independent parts, one for each index of `groups`. The reference program is written for one: setup_inputs(seed, part) draws one part's arguments, and reference() takes and returns one part's arrays. A program takes and returns all parts, laid end to end along the dimension named above; an argument that names none is the same for every part. Nothing has to cross between parts.
Inputs may be any that keep to these rules, and one draw needn't show every extreme that they name: `tile_vals`: entries are zero or positive. `tile_cols`: entry s of row block b names a row block held by the device of b or by one of the two devices beside it on the closed loop of devices along dom; the 24 entries of a row block are distinct; only the first tile_count[b] are read. `tile_count`: one part's values sum to 1536. `bound_ids`: of the 1024 entries of one device's row blocks, at most 128 fall in the 64 rows of hist_cache held by any one device, and exactly 128 in those of some device.
All inputs are finite; a program needn't handle non-finite values. No bound on the sum of `tile_count` on one device may be relied on, other than what follows from the above.
Results may differ from the reference program's by a relative error of at most 0.0095.
Values may be sent and summed in bfloat16 or wider, within the bound.
A program may use at most 64 MiB of HBM per device.

```python
import math
import jax
import jax.numpy as jnp
import numpy as np
from jax import lax

F = 256
BLK = 128
RB_DEV = 8
BND = 128
HIST_DEV = 64
SLOTS = 24
NB = 128
NODES = 16384
HIST = 1024


def draw_tile_vals(key, part):
    key = jax.random.fold_in(key, 11)
    key_mask, key_val, key_row, key_col = jax.random.split(key, 4)
    full_shape = (NB, SLOTS, BLK, BLK)
    keep_mask = jax.random.bernoulli(key_mask, 0.25, full_shape).astype(jnp.float32)
    values = jnp.exp(jax.random.uniform(key_val, full_shape, jnp.float32, -2.302, 0.0))
    row_scale = jnp.exp(jax.random.uniform(key_row, (NB, 1, BLK, 1), jnp.float32, -1.151, 1.151))
    col_scale = jnp.exp(jax.random.uniform(key_col, (NB, SLOTS, 1, BLK), jnp.float32, -1.151, 1.151))
    return (keep_mask * values * row_scale * col_scale).astype(jnp.bfloat16)


def draw_tile_cols(key, part):
    key = jax.random.fold_in(key, 23)
    row_keys = jax.random.split(key, NB)
    band_pos = jax.vmap(lambda dev_key: jax.random.permutation(dev_key, SLOTS))(row_keys).astype(jnp.int32)
    devices = NB // RB_DEV
    home_dev = (jnp.arange(NB, dtype=jnp.int32) // RB_DEV)[:, None]
    owner_dev = jnp.mod(home_dev - 1 + band_pos // RB_DEV, devices)
    return (owner_dev * RB_DEV + band_pos % RB_DEV).astype(jnp.int32)


def draw_bound_ids(key, part):
    key = jax.random.fold_in(key, 37)
    devices = NB // RB_DEV
    ref_count = RB_DEV * BND
    capacity = 2 * ref_count // devices

    def one_device(dev_key):
        key_top, key_rest, key_order, key_row = jax.random.split(dev_key, 4)
        busiest = jax.random.randint(key_top, (), 0, devices)
        others = jax.random.permutation(key_rest, (devices - 1) * capacity)[:ref_count - capacity] // capacity
        owners = jnp.concatenate([jnp.full((capacity,), busiest, jnp.int32), jnp.mod(busiest + 1 + others, devices).astype(jnp.int32)])
        owners = owners[jax.random.permutation(key_order, ref_count)]
        offsets = jax.random.randint(key_row, (ref_count,), 0, HIST_DEV)
        return owners * HIST_DEV + offsets
    drawn_ids = jax.vmap(one_device)(jax.random.split(key, devices))
    return drawn_ids.reshape(NB, BND).astype(jnp.int32)


def block_scale(rng, extent, pieces, low, high):
    level, own = 1.0, jax.random.fold_in(rng, 6)
    for dim, shards_of in pieces:
        heights = jnp.exp(jax.random.uniform(jax.random.fold_in(own, dim), (shards_of,), jnp.float32, low / len(pieces), high / len(pieces)))
        level = level * jnp.repeat(heights, extent[dim] // shards_of).reshape([-1 if axis == dim else 1 for axis in range(len(extent))])
    return level


def split_up(count, total, most, skew):
    weights = [(1 << 20) // math.isqrt(grade ** skew) + 1 for grade in range(2, count + 1)]
    spare, holding = total - most - (count - 1), [1] * (count - 1)
    while spare > 0:
        candidates = [i for i in range(count - 1) if holding[i] < most]
        mass, left = sum([weights[i] for i in candidates]), spare
        for i in candidates:
            extra = min(most - holding[i], max(1, left * weights[i] // mass), spare)
            holding[i] = holding[i] + extra
            spare = spare - extra
    return np.array([most] + holding)


def ragged(own_key, amount, total, reach, slope):
    if amount == 2:
        one = jax.random.randint(own_key, (), max(1, total - reach), min(reach, total - 1) + 1)
        return jnp.stack([one, total - one])
    tallies = jnp.asarray(split_up(amount, total, reach, slope), jnp.int32)
    pairs = (amount - 1) // 2
    donor, taker = tallies[1:1 + 2 * pairs:2], tallies[2:2 + 2 * pairs:2]
    room = jnp.minimum(donor - 1, reach - taker)
    shifted = jax.random.randint(jax.random.fold_in(own_key, 1), (pairs,), 0, 1 << 20) % (room + 1)
    tallies = tallies.at[1:1 + 2 * pairs:2].set(donor - shifted).at[2:2 + 2 * pairs:2].set(taker + shifted)
    return tallies[jax.random.permutation(jax.random.fold_in(own_key, 2), amount)]


def noise(key, shape, deviation, reach, shards=(), kind=jnp.bfloat16):
    level = block_scale(key, shape, shards, -0.22, 0.18) if shards else 1.0
    array = jax.random.normal(key, shape, jnp.float32) * deviation * level
    return jnp.minimum(jnp.maximum(array, -reach), reach).astype(kind)


def setup_inputs(seed: int = 0, part: int = 0) -> dict:
    splits = jax.random.split(jax.random.key(seed), 12)
    own_keys = jax.random.split(jax.random.fold_in(splits[11], part), 12)
    node_feats = noise(own_keys[0], (NODES, F), 1.0, 6.0, ((0, 16),))
    tile_vals = draw_tile_vals(jax.random.fold_in(jax.random.fold_in(splits[11], part), 71), part)
    tile_cols = draw_tile_cols(jax.random.fold_in(jax.random.fold_in(splits[11], part), 71), part)
    tile_count = ragged(own_keys[3], NB, NB * SLOTS // 2, SLOTS, 2).astype(jnp.int32)
    hist_cache = noise(own_keys[4], (HIST, F), 1.0, 6.0, ((0, 16),))
    bound_ids = draw_bound_ids(jax.random.fold_in(jax.random.fold_in(splits[11], part), 71), part)
    bound_wts = jnp.clip(jnp.exp(math.log(1.0) - 2.9996462 * jax.random.uniform(own_keys[6], (NODES, BND), jnp.float32) ** block_scale(own_keys[6], (NODES, BND), ((0, 16),), -0.2, 0.2)), 0.049804688, 1.0).astype(jnp.bfloat16)
    w_self = noise(splits[7], (F, F), F ** -0.5, 0.375)
    w_neigh = noise(splits[8], (F, F), 1.0, 6.0)
    out_bias = noise(splits[9], (F,), 0.5, 3.0, (), jnp.float32)
    out_grad = noise(own_keys[10], (NODES, F), 1.0, 6.0, ((0, 16),))
    return {"node_feats": node_feats, "tile_vals": tile_vals, "tile_cols": tile_cols, "tile_count": tile_count, "hist_cache": hist_cache, "bound_ids": bound_ids, "bound_wts": bound_wts, "w_self": w_self, "w_neigh": w_neigh, "out_bias": out_bias, "out_grad": out_grad}


def reference(node_feats, tile_vals, tile_cols, tile_count, hist_cache, bound_ids, bound_wts, w_self, w_neigh, out_bias, out_grad):
    feat_blocks = node_feats.reshape(NB, BLK, F)
    live_mask = (jnp.arange(SLOTS, dtype=jnp.int32)[None, :] < tile_count[:, None]).astype(jnp.float32)
    row_sums = lax.optimization_barrier(jnp.sum(tile_vals, axis=3, dtype=jnp.float32))
    bound_sums = lax.optimization_barrier(jnp.sum(bound_wts, axis=1, dtype=jnp.float32)).reshape(NB, BLK)
    degrees = 1.0 + jnp.einsum('bs,bsi->bi', live_mask, row_sums, precision=lax.Precision.HIGHEST) + bound_sums
    hist_rows = jnp.take(hist_cache, bound_ids, axis=0)
    wts_blocks = bound_wts.reshape(NB, BLK, BND)

    def gather_block(operands):
        tile_block, columns, slot_mask, weights, cached = operands
        sources = jnp.take(feat_blocks, columns, axis=0).astype(jnp.float32)
        weighted = tile_block.astype(jnp.float32) * slot_mask[:, None, None]
        summed = jnp.einsum('sij,sjf->if', weighted, sources, precision=lax.Precision.HIGHEST)
        return summed + jnp.einsum('im,mf->if', weights.astype(jnp.float32), cached.astype(jnp.float32), precision=lax.Precision.HIGHEST)
    numerator = lax.map(gather_block, (tile_vals, tile_cols, live_mask, wts_blocks, hist_rows))
    aggregated = (numerator / degrees[:, :, None]).reshape(NODES, F).astype(jnp.bfloat16)
    pre_act = jnp.dot(node_feats, w_self, preferred_element_type=jnp.float32) + jnp.dot(aggregated, w_neigh, preferred_element_type=jnp.float32) + out_bias[None, :]
    sigmoid_of = jax.nn.sigmoid(pre_act)
    hidden_out = (pre_act * sigmoid_of).astype(jnp.bfloat16)
    dz_rows = (out_grad.astype(jnp.float32) * sigmoid_of * (1.0 + pre_act * (1.0 - sigmoid_of))).astype(jnp.bfloat16)
    inv_scale = 1.0 / math.sqrt(NODES)
    self_grad = jnp.dot(node_feats.T, dz_rows, preferred_element_type=jnp.float32) * inv_scale
    neigh_grad = jnp.dot(aggregated.T, dz_rows, preferred_element_type=jnp.float32) * inv_scale
    bias_grad = lax.optimization_barrier(jnp.sum(dz_rows.astype(jnp.float32), axis=0)) * inv_scale
    back_neigh = lax.dot_general(dz_rows, w_neigh, (((1,), (1,)), ((), ())), preferred_element_type=jnp.float32)
    scaled = (back_neigh.reshape(NB, BLK, F) / degrees[:, :, None]).astype(jnp.bfloat16)

    def spread_block(totals, operands):
        tile_block, columns, slot_mask, grad_rows = operands
        weighted = tile_block.astype(jnp.float32) * slot_mask[:, None, None]
        tile_terms = jnp.einsum('sij,if->sjf', weighted, grad_rows.astype(jnp.float32), precision=lax.Precision.HIGHEST)
        return (totals.at[columns].add(tile_terms), None)
    spread = lax.scan(spread_block, jnp.zeros((NB, BLK, F), jnp.float32), (tile_vals, tile_cols, live_mask, scaled))[0]
    self_back = lax.dot_general(dz_rows, w_self, (((1,), (1,)), ((), ())), preferred_element_type=jnp.float32)
    feat_grad = (self_back + spread.reshape(NODES, F)).astype(jnp.bfloat16)
    return (hidden_out, feat_grad, self_grad, neigh_grad, bias_grad)
```

```python
import functools
import math

import jax
import jax.numpy as jnp
from jax import lax
from jax.experimental import pallas as pl
from jax.experimental.pallas import tpu as pltpu
from jax.sharding import PartitionSpec as P

MESH = pl.DeviceIdType.MESH
F32 = jnp.float32
BF16 = jnp.bfloat16
NN = (((1,), (0,)), ((), ()))
NT = (((1,), (1,)), ((), ()))
TN = (((0,), (0,)), ((), ()))


def mm(a, b, dims):
    return lax.dot_general(a, b, dims, preferred_element_type=F32)


def layer_kernel(
    count,
    code_ref,
    ids_ref,
    wts_ref,
    ws_ref,
    wn_ref,
    bias_ref,
    og_ref,
    x_hbm,
    hist_hbm,
    tiles_hbm,
    hid_ref,
    feat_ref,
    gself_ref,
    gneigh_ref,
    gbias_ref,
    tiles,
    band,
    ext,
    rdeg,
    base,
    dz_s,
    agg_s,
    scaled_t,
    own_t,
    out_l,
    out_r,
    in_l,
    in_r,
    gsend,
    grecv,
    gfin,
    brow,
    local_sem,
    halo_sem,
    back_sem,
    hist_send,
    hist_recv,
    fwd_send,
    fwd_recv,
    rs_send,
    rs_recv,
    ag_send,
    ag_recv,
):
    rows = x_hbm.shape[0]
    feat = x_hbm.shape[1]
    row_blocks, slots, tile, _ = tiles.shape
    hrows = hist_hbm.shape[0]
    hist = count * hrows
    hbase = 3 * rows
    pairs = count // 2
    chunk = gfin.shape[1]
    inv_scale = 1.0 / math.sqrt(count * rows)

    me = lax.axis_index("dom")
    right = lax.rem(me + 1, count)
    left = lax.rem(me + count - 1, count)
    partner = me + 1 - 2 * lax.rem(me, 2)

    def remote(src, dst, send, recv, peer):
        return pltpu.make_async_remote_copy(
            src_ref=src,
            dst_ref=dst,
            send_sem=send,
            recv_sem=recv,
            device_id={"dom": peer},
            device_id_type=MESH,
        )

    barrier = pltpu.get_barrier_semaphore()

    @pl.loop(1, count)
    def _(d):
        pl.semaphore_signal(
            barrier, inc=1, device_id={"dom": lax.rem(me + d, count)}, device_id_type=MESH
        )

    own_rows = pl.ds(pl.multiple_of(hbase + me * hrows, hrows), hrows)
    tile_copy = pltpu.make_async_copy(tiles_hbm, tiles, local_sem.at[0])
    tile_copy.start()
    x_copy = pltpu.make_async_copy(x_hbm, ext.at[pl.ds(rows, rows)], local_sem.at[1])
    x_copy.start()
    h_copy = pltpu.make_async_copy(hist_hbm, ext.at[own_rows], local_sem.at[2])
    h_copy.start()

    pl.semaphore_wait(barrier, count - 1)

    def hist_copy(k):
        return remote(
            hist_hbm,
            ext.at[own_rows],
            hist_send.at[k],
            hist_recv.at[k],
            lax.rem(me + 2 * k, count),
        )

    def fwd_copy(k):
        src = lax.rem(me + count - 2 * k, count)
        at = pl.ds(pl.multiple_of(hbase + src * hrows, hrows), hrows)
        return remote(ext.at[at], ext.at[at], fwd_send.at[k], fwd_recv.at[k], partner)

    first = remote(hist_hbm, ext.at[own_rows], fwd_send.at[0], fwd_recv.at[0], partner)
    first.start()

    @pl.loop(1, pairs)
    def _(k):
        hist_copy(k).start()

    to_right = remote(
        x_hbm, ext.at[pl.ds(0, rows)], halo_sem.at[0], halo_sem.at[1], right
    )
    to_left = remote(
        x_hbm, ext.at[pl.ds(2 * rows, rows)], halo_sem.at[2], halo_sem.at[3], left
    )
    to_right.start()
    to_left.start()

    hstep = min(hist, 512)

    @pl.loop(0, row_blocks)
    def _(b):
        at = pl.ds(pl.multiple_of(b * tile, tile), tile)
        ids = ids_ref[pl.ds(b, 1), :]
        wts = wts_ref[at, :]
        for h in range(0, hist, hstep):
            hot = lax.broadcasted_iota(jnp.int32, (hstep, tile), 0) + h == ids
            hot = jnp.where(hot, 1.0, 0.0).astype(BF16)
            band[at, hbase + h : hbase + h + hstep] = mm(wts, hot, NT).astype(BF16)

    tile_copy.wait()
    x_copy.wait()
    h_copy.wait()

    @pl.loop(0, row_blocks)
    def _(b):
        at = pl.ds(pl.multiple_of(b * tile, tile), tile)
        total = wts_ref[at, :].astype(F32)
        for p in range(slots):
            code = code_ref[b, p]
            live = jnp.where(code >= 0, 1.0, 0.0)
            part = tiles[b, jnp.maximum(code, 0)].astype(F32) * live
            total = total + part
            band[at, p * tile : (p + 1) * tile] = part.astype(BF16)
        degree = 1.0 + jnp.sum(total, axis=1, keepdims=True)
        rdeg[at, :] = jnp.broadcast_to(1.0 / degree, (tile, feat))

    step = 256

    @pl.loop(1, pairs)
    def _(k):
        hist_copy(k).wait_recv()
        fwd_copy(k).start()

    @pl.loop(0, rows // step)
    def _(r):
        at = pl.ds(pl.multiple_of(r * step, step), step)
        base[at, :] = mm(band[at, rows : 2 * rows], ext[rows : 2 * rows, :], NN)

    first.wait_recv()

    @pl.loop(1, pairs)
    def _(k):
        fwd_copy(k).wait_recv()

    @pl.loop(0, rows // step)
    def _(r):
        at = pl.ds(pl.multiple_of(r * step, step), step)
        base[at, :] += mm(band[at, hbase:], ext[hbase:, :], NN)

    to_right.wait_recv()
    to_left.wait_recv()

    @pl.loop(0, rows // step)
    def _(r):
        at = pl.ds(pl.multiple_of(r * step, step), step)
        num = (
            base[at, :]
            + mm(band[at, :rows], ext[:rows, :], NN)
            + mm(band[at, 2 * rows : hbase], ext[2 * rows : hbase, :], NN)
        )
        recip = rdeg[at, :]
        agg = (num * recip).astype(BF16)
        x = ext[pl.ds(pl.multiple_of(rows + r * step, step), step), :]
        pre = mm(x, ws_ref[...], NN) + mm(agg, wn_ref[...], NN) + bias_ref[...]
        sig = jax.nn.sigmoid(pre)
        hid_ref[at, :] = (pre * sig).astype(BF16)
        dz = (og_ref[at, :].astype(F32) * sig * (1.0 + pre * (1.0 - sig))).astype(BF16)
        scaled = mm(dz, wn_ref[...], NT) * recip
        agg_s[at, :] = agg
        dz_s[at, :] = dz
        scaled_t[:, at] = scaled.T.astype(BF16)

    back_left = remote(out_l, in_r, back_sem.at[0], back_sem.at[1], left)
    back_right = remote(out_r, in_l, back_sem.at[2], back_sem.at[3], right)
    out_l[...] = mm(scaled_t[...], band[:, :rows], NN).astype(BF16)
    back_left.start()
    out_r[...] = mm(scaled_t[...], band[:, 2 * rows : hbase], NN).astype(BF16)
    back_right.start()

    dz = dz_s[...]
    bias_sum = jnp.sum(dz.astype(F32), axis=0, keepdims=True)
    high = bias_sum.astype(BF16).astype(F32)
    low = bias_sum - high
    row = lax.broadcasted_iota(jnp.int32, (16, 128), 0)
    zero = jnp.zeros((16, 128), F32)
    bias_rows = jnp.where(
        row == 0,
        high[:, :128],
        jnp.where(
            row == 1,
            high[:, 128:],
            jnp.where(row == 2, low[:, :128], jnp.where(row == 3, low[:, 128:], zero)),
        ),
    ).astype(BF16)
    grads = (mm(ext[rows : 2 * rows, :], dz, TN), mm(agg_s[...], dz, TN))
    for j in range(count):
        quarter, start = divmod(j * chunk, feat)
        half = (quarter % 2) * 128
        part = grads[quarter // 2][start : start + chunk, half : half + 128]
        gsend[j, :chunk, :] = part.astype(BF16)
        gsend[j, chunk:, :] = bias_rows

    def rs_copy(d):
        peer = lax.rem(me + d, count)
        return remote(gsend.at[peer], grecv.at[me], rs_send.at[d], rs_recv.at[d], peer)

    def ag_copy(d):
        peer = lax.rem(me + d, count)
        return remote(gfin.at[me], gfin.at[me], ag_send.at[d], ag_recv.at[d], peer)

    @pl.loop(1, count)
    def _(d):
        rs_copy(d).start()

    own_t[...] = mm(scaled_t[...], band[:, rows : 2 * rows], NN)

    @pl.loop(0, rows // step)
    def _(r):
        at = pl.ds(pl.multiple_of(r * step, step), step)
        base[at, :] = mm(dz_s[at, :], ws_ref[...], NT)

    @pl.loop(1, count)
    def _(d):
        rs_copy(d).wait_recv()

    def add(d, total):
        return total + grecv[lax.rem(me + d, count)].astype(F32)

    total = lax.fori_loop(1, count, add, gsend[me].astype(F32))
    gfin[me] = (total[:chunk] * inv_scale).astype(BF16)

    @pl.loop(1, count)
    def _(d):
        ag_copy(d).start()

    brow[...] = total[chunk:] * inv_scale
    gbias_ref[...] = brow[0:2, :] + brow[2:4, :]

    back_left.wait_recv()
    back_right.wait_recv()

    @pl.loop(0, rows // step)
    def _(r):
        at = pl.ds(pl.multiple_of(r * step, step), step)
        spread = own_t[:, at] + in_l[:, at].astype(F32) + in_r[:, at].astype(F32)
        feat_ref[at, :] = (base[at, :] + spread.T).astype(BF16)

    @pl.loop(1, count)
    def _(d):
        ag_copy(d).wait_recv()

    for j in range(count):
        quarter, start = divmod(j * chunk, feat)
        half = (quarter % 2) * 128
        out = gself_ref if quarter < 2 else gneigh_ref
        out[start : start + chunk, half : half + 128] = gfin[j].astype(F32)

    first.wait_send()
    to_right.wait_send()
    to_left.wait_send()
    back_left.wait_send()
    back_right.wait_send()

    @pl.loop(1, pairs)
    def _(k):
        hist_copy(k).wait_send()
        fwd_copy(k).wait_send()

    @pl.loop(1, count)
    def _(d):
        rs_copy(d).wait_send()
        ag_copy(d).wait_send()


def body(
    node_feats,
    tile_vals,
    tile_cols,
    tile_count,
    hist_cache,
    bound_ids,
    bound_wts,
    w_self,
    w_neigh,
    out_bias,
    out_grad,
):
    row_blocks, slots, tile, _ = tile_vals.shape
    rows, feat = node_feats.shape
    count = lax.axis_size("dom")
    me = lax.axis_index("dom")
    hist = count * hist_cache.shape[0]
    chunk = 2 * feat * feat // (128 * count)

    offset = jnp.mod(tile_cols // row_blocks - me + 1, count)
    positions = offset * row_blocks + tile_cols % row_blocks
    slot_ids = jnp.arange(slots, dtype=jnp.int32)
    here = (positions[:, :, None] == slot_ids[None, None, :]) & (
        slot_ids[None, :, None] < tile_count[:, None, None]
    )
    code = jnp.sum(jnp.where(here, slot_ids[None, :, None] + 1, 0), axis=1) - 1

    vmem = pl.BlockSpec(memory_space=pltpu.VMEM)
    anywhere = pl.BlockSpec(memory_space=pl.ANY)
    dma = pltpu.SemaphoreType.DMA
    outs = pl.pallas_call(
        functools.partial(layer_kernel, count),
        out_shape=(
            jax.ShapeDtypeStruct((rows, feat), BF16),
            jax.ShapeDtypeStruct((rows, feat), BF16),
            jax.ShapeDtypeStruct((feat, feat), F32),
            jax.ShapeDtypeStruct((feat, feat), F32),
            jax.ShapeDtypeStruct((2, feat // 2), F32),
        ),
        in_specs=[pl.BlockSpec(memory_space=pltpu.SMEM)] + [vmem] * 6 + [anywhere] * 3,
        out_specs=(vmem,) * 5,
        scratch_shapes=[
            pltpu.VMEM(tile_vals.shape, BF16),
            pltpu.VMEM((rows, 3 * rows + hist), BF16),
            pltpu.VMEM((3 * rows + hist, feat), BF16),
            pltpu.VMEM((rows, feat), F32),
            pltpu.VMEM((rows, feat), F32),
            pltpu.VMEM((rows, feat), BF16),
            pltpu.VMEM((rows, feat), BF16),
            pltpu.VMEM((feat, rows), BF16),
            pltpu.VMEM((feat, rows), F32),
            pltpu.VMEM((feat, rows), BF16),
            pltpu.VMEM((feat, rows), BF16),
            pltpu.VMEM((feat, rows), BF16),
            pltpu.VMEM((feat, rows), BF16),
            pltpu.VMEM((count, chunk + 16, 128), BF16),
            pltpu.VMEM((count, chunk + 16, 128), BF16),
            pltpu.VMEM((count, chunk, 128), BF16),
            pltpu.VMEM((16, 128), F32),
            dma((3,)),
            dma((4,)),
            dma((4,)),
            dma((count // 2,)),
            dma((count // 2,)),
            dma((count // 2,)),
            dma((count // 2,)),
            dma((count,)),
            dma((count,)),
            dma((count,)),
            dma((count,)),
        ],
        compiler_params=pltpu.CompilerParams(
            collective_id=0, has_side_effects=True, vmem_limit_bytes=56 * 1024 * 1024
        ),
    )(
        code,
        bound_ids,
        bound_wts,
        w_self,
        w_neigh,
        out_bias.reshape(1, feat),
        out_grad,
        node_feats,
        hist_cache,
        tile_vals,
    )
    return outs[:4] + (outs[4].reshape(feat),)


def solution(mesh):
    placed = (
        P(("groups", "dom"), None),
        P(("groups", "dom"), None, None, None),
        P(("groups", "dom"), None),
        P(("groups", "dom")),
        P(("groups", "dom"), None),
        P(("groups", "dom"), None),
        P(("groups", "dom"), None),
        P(),
        P(),
        P(),
        P(("groups", "dom"), None),
    )
    return jax.shard_map(
        body,
        mesh=mesh,
        in_specs=placed,
        out_specs=(
            P(("groups", "dom"), None),
            P(("groups", "dom"), None),
            P("groups", None),
            P("groups", None),
            P("groups"),
        ),
        check_vma=False,
    )
```

```python
import functools
import math

import jax
import jax.numpy as jnp
from jax import lax
from jax.experimental import pallas as pl
from jax.experimental.pallas import tpu as pltpu
from jax.sharding import PartitionSpec as P

MESH = pl.DeviceIdType.MESH
F32 = jnp.float32
BF16 = jnp.bfloat16
NN = (((1,), (0,)), ((), ()))
NT = (((1,), (1,)), ((), ()))
TN = (((0,), (0,)), ((), ()))


def mm(a, b, dims):
    return lax.dot_general(a, b, dims, preferred_element_type=F32)


def layer_kernel(
    count,
    live_ref,
    cols_ref,
    ids_ref,
    bias_ref,
    wts_hbm,
    ws_hbm,
    wn_hbm,
    og_hbm,
    x_hbm,
    hist_hbm,
    tiles_hbm,
    hid_ref,
    feat_ref,
    gself_ref,
    gneigh_ref,
    gbias_ref,
    wts_ref,
    ws_ref,
    wn_ref,
    og_ref,
    tiles,
    band,
    ext,
    rdeg,
    base,
    pre_s,
    dz_s,
    agg_s,
    scaled_t,
    own_t,
    out_far,
    out_near,
    in_far,
    in_near,
    gsend,
    gpair,
    gsum,
    grecv,
    gfin,
    brow,
    code_vec,
    code_ref,
    local_sem,
    halo_send,
    halo_recv,
    back_send,
    back_recv,
    hist_send,
    hist_recv,
    fwd_send,
    fwd_recv,
    pair_sem,
    rs_send,
    rs_recv,
    ag_send,
    ag_recv,
    agf_send,
    agf_recv,
):
    rows = x_hbm.shape[0]
    feat = x_hbm.shape[1]
    row_blocks, slots, tile, _ = tiles.shape
    hrows = hist_hbm.shape[0]
    hist = count * hrows
    hbase = 3 * rows
    pairs = count // 2
    chunk = gfin.shape[1]
    inv_scale = 1.0 / math.sqrt(count * rows)
    step = 256
    half = rows // 2

    me = lax.axis_index("dom")
    side = lax.rem(me, 2)
    partner = me + 1 - 2 * side
    far = lax.rem(me + count - 1 + 2 * side, count)

    def peer_of(k):
        return lax.rem(me + 2 * k, count)

    def source_of(k):
        return lax.rem(me + count - 2 * k, count)

    def remote(src, dst, send, recv, peer):
        return pltpu.make_async_remote_copy(
            src_ref=src,
            dst_ref=dst,
            send_sem=send,
            recv_sem=recv,
            device_id={"dom": peer},
            device_id_type=MESH,
        )

    def greet(peer):
        pl.semaphore_signal(barrier, inc=1, device_id={"dom": peer}, device_id_type=MESH)

    barrier = pltpu.get_barrier_semaphore()
    greet(far)
    greet(partner)

    @pl.loop(1, pairs)
    def _(k):
        greet(peer_of(k))

    own_rows = pl.ds(pl.multiple_of(hbase + me * hrows, hrows), hrows)
    pieces = (
        (wts_hbm, wts_ref),
        (hist_hbm, ext.at[own_rows]),
        (x_hbm, ext.at[pl.ds(rows, rows)]),
        (ws_hbm, ws_ref),
        (wn_hbm, wn_ref),
        (tiles_hbm, tiles),
        (og_hbm, og_ref),
    )
    loads = [pltpu.make_async_copy(a, b, local_sem.at[i]) for i, (a, b) in enumerate(pieces)]
    for load in loads:
        load.start()

    pl.semaphore_wait(barrier, pairs + 1)

    far_there = (1 - side) * 2 * rows
    near_there = side * 2 * rows
    far_here = side * 2 * rows
    near_here = (1 - side) * 2 * rows

    def halo_far(j):
        at = pl.ds(pl.multiple_of(far_there + j * half, half), half)
        return remote(
            x_hbm.at[pl.ds(j * half, half)], ext.at[at], halo_send.at[j], halo_recv.at[j], far
        )

    halo_near = remote(
        x_hbm,
        ext.at[pl.ds(pl.multiple_of(near_there, rows), rows)],
        halo_send.at[2],
        halo_recv.at[2],
        partner,
    )

    def hist_copy(k):
        return remote(
            hist_hbm, ext.at[own_rows], hist_send.at[k], hist_recv.at[k], peer_of(k)
        )

    def fwd_copy(k):
        at = pl.ds(pl.multiple_of(hbase + source_of(k) * hrows, hrows), hrows)
        return remote(ext.at[at], ext.at[at], fwd_send.at[k], fwd_recv.at[k], partner)

    first = remote(hist_hbm, ext.at[own_rows], fwd_send.at[0], fwd_recv.at[0], partner)

    @pl.loop(1, pairs)
    def _(k):
        hist_copy(k).start()

    halo_far(0).start()
    halo_far(1).start()
    first.start()
    halo_near.start()

    blocks = count * row_blocks
    pos = cols_ref[...] - (me - 1) * row_blocks
    pos = jnp.where(pos < 0, pos + blocks, jnp.where(pos >= blocks, pos - blocks, pos))
    block_of = lax.broadcasted_iota(jnp.int32, code_vec.shape, 0)
    place = lax.broadcasted_iota(jnp.int32, code_vec.shape, 1)
    limit = jnp.zeros(code_vec.shape, jnp.int32)
    for b in range(row_blocks):
        limit = jnp.where(block_of == b, live_ref[b], limit)
    code = jnp.full(code_vec.shape, -1, jnp.int32)
    for s in range(slots):
        code = jnp.where((pos[:, s : s + 1] == place) & (limit > s), s, code)
    code_vec[...] = code
    code_copy = pltpu.make_async_copy(code_vec, code_ref, local_sem.at[len(pieces)])
    code_copy.start()

    hstep = min(hist, 512)
    loads[0].wait()

    @pl.loop(0, row_blocks)
    def _(b):
        at = pl.ds(pl.multiple_of(b * tile, tile), tile)
        ids = ids_ref[pl.ds(b, 1), :]
        wts = wts_ref[at, :]
        for h in range(0, hist, hstep):
            hot = lax.broadcasted_iota(jnp.int32, (hstep, tile), 0) + h == ids
            hot = jnp.where(hot, 1.0, 0.0).astype(BF16)
            band[at, hbase + h : hbase + h + hstep] = mm(wts, hot, NT).astype(BF16)

    for load in loads[1:]:
        load.wait()
    code_copy.wait()

    @pl.loop(0, row_blocks)
    def _(b):
        at = pl.ds(pl.multiple_of(b * tile, tile), tile)
        total = wts_ref[at, :].astype(F32)
        for p in range(slots):
            code = code_ref[b, p]
            live = jnp.where(code >= 0, 1.0, 0.0)
            part = tiles[b, jnp.maximum(code, 0)].astype(F32) * live
            total = total + part
            band[at, p * tile : (p + 1) * tile] = part.astype(BF16)
        degree = 1.0 + jnp.sum(total, axis=1, keepdims=True)
        rdeg[at, :] = jnp.broadcast_to(1.0 / degree, (tile, feat))

    @pl.loop(1, pairs)
    def _(k):
        hist_copy(k).wait_recv()
        fwd_copy(k).start()

    @pl.loop(0, rows // step)
    def _(r):
        at = pl.ds(pl.multiple_of(r * step, step), step)
        own = ext[pl.ds(pl.multiple_of(rows + r * step, step), step), :]
        base[at, :] = mm(band[at, rows : 2 * rows], ext[rows : 2 * rows, :], NN)
        pre_s[at, :] = mm(own, ws_ref[...], NN) + bias_ref[...]

    halo_near.wait_recv()
    first.wait_recv()

    @pl.loop(1, pairs)
    def _(k):
        fwd_copy(k).wait_recv()

    near_at = pl.ds(pl.multiple_of(near_here, rows), rows)
    far_at = pl.ds(pl.multiple_of(far_here, rows), rows)
    far_half = [pl.ds(pl.multiple_of(far_here + j * half, half), half) for j in range(2)]

    @pl.loop(0, rows // step)
    def _(r):
        at = pl.ds(pl.multiple_of(r * step, step), step)
        base[at, :] += mm(band[at, hbase:], ext[hbase:, :], NN) + mm(
            band[at, near_at], ext[near_at, :], NN
        )

    halo_far(0).wait_recv()

    @pl.loop(0, rows // step)
    def _(r):
        at = pl.ds(pl.multiple_of(r * step, step), step)
        base[at, :] += mm(band[at, far_half[0]], ext[far_half[0], :], NN)

    halo_far(1).wait_recv()

    @pl.loop(0, rows // step)
    def _(r):
        at = pl.ds(pl.multiple_of(r * step, step), step)
        num = base[at, :] + mm(band[at, far_half[1]], ext[far_half[1], :], NN)
        recip = rdeg[at, :]
        agg = (num * recip).astype(BF16)
        pre = pre_s[at, :] + mm(agg, wn_ref[...], NN)
        sig = jax.nn.sigmoid(pre)
        hid_ref[at, :] = (pre * sig).astype(BF16)
        dz = (og_ref[at, :].astype(F32) * sig * (1.0 + pre * (1.0 - sig))).astype(BF16)
        scaled = mm(dz, wn_ref[...], NT) * recip
        agg_s[at, :] = agg
        dz_s[at, :] = dz
        scaled_t[:, at] = scaled.T.astype(BF16)

    dz = dz_s[...]
    bias_sum = jnp.sum(dz.astype(F32), axis=0, keepdims=True)
    row = lax.broadcasted_iota(jnp.int32, (16, 128), 0)
    bias_rows = jnp.where(
        row == 0, bias_sum[:, :128], jnp.where(row == 1, bias_sum[:, 128:], 0.0)
    ).astype(BF16)
    grads = (mm(ext[rows : 2 * rows, :], dz, TN), mm(agg_s[...], dz, TN))
    for j in range(count):
        quarter, start = divmod(j * chunk, feat)
        lanes = (quarter % 2) * 128
        part = grads[quarter // 2][start : start + chunk, lanes : lanes + 128]
        gsend[j % 2, j // 2, :chunk, :] = part.astype(BF16)
        gsend[j % 2, j // 2, chunk:, :] = bias_rows

    pair_copy = remote(gsend.at[1 - side], gpair, pair_sem.at[0], pair_sem.at[1], partner)
    pair_copy.start()

    back_far = remote(out_far, in_far, back_send.at[0], back_recv.at[0], far)
    back_near = remote(out_near, in_near, back_send.at[1], back_recv.at[1], partner)
    out_far[...] = mm(scaled_t[...], band[:, far_at], NN).astype(BF16)
    back_far.start()

    chip = me // 2

    def rs_copy(k):
        peer = peer_of(k)
        return remote(
            gsum.at[peer // 2], grecv.at[chip], rs_send.at[k], rs_recv.at[k], peer
        )

    def ag_copy(k):
        return remote(gfin.at[me], gfin.at[me], ag_send.at[k], ag_recv.at[k], peer_of(k))

    def agf_copy(k):
        src = source_of(k)
        return remote(gfin.at[src], gfin.at[src], agf_send.at[k], agf_recv.at[k], partner)

    pair_copy.wait_recv()
    gsum[...] = (gsend[side].astype(F32) + gpair[...].astype(F32)).astype(BF16)

    @pl.loop(1, pairs)
    def _(k):
        rs_copy(k).start()

    out_near[...] = mm(scaled_t[...], band[:, near_at], NN).astype(BF16)
    back_near.start()
    own_t[...] = mm(scaled_t[...], band[:, rows : 2 * rows], NN)

    @pl.loop(0, rows // step)
    def _(r):
        at = pl.ds(pl.multiple_of(r * step, step), step)
        base[at, :] = mm(dz_s[at, :], ws_ref[...], NT)

    @pl.loop(1, pairs)
    def _(k):
        rs_copy(k).wait_recv()

    def add(k, total):
        return total + grecv[lax.rem(chip + k, pairs)].astype(F32)

    total = lax.fori_loop(1, pairs, add, gsum[chip].astype(F32))
    gfin[me] = (total[:chunk] * inv_scale).astype(BF16)
    agf_first = agf_copy(0)
    agf_first.start()

    @pl.loop(1, pairs)
    def _(k):
        ag_copy(k).start()

    brow[...] = total[chunk:] * inv_scale
    gbias_ref[...] = brow[0:2, :]

    @pl.loop(1, pairs)
    def _(k):
        ag_copy(k).wait_recv()
        agf_copy(k).start()

    back_near.wait_recv()
    back_far.wait_recv()

    @pl.loop(0, rows // step)
    def _(r):
        at = pl.ds(pl.multiple_of(r * step, step), step)
        spread = own_t[:, at] + in_near[:, at].astype(F32) + in_far[:, at].astype(F32)
        feat_ref[at, :] = (base[at, :] + spread.T).astype(BF16)

    agf_first.wait_recv()

    @pl.loop(1, pairs)
    def _(k):
        agf_copy(k).wait_recv()

    for j in range(count):
        quarter, start = divmod(j * chunk, feat)
        lanes = (quarter % 2) * 128
        out = gself_ref if quarter < 2 else gneigh_ref
        out[start : start + chunk, lanes : lanes + 128] = gfin[j].astype(F32)

    first.wait_send()
    halo_far(0).wait_send()
    halo_far(1).wait_send()
    halo_near.wait_send()
    back_far.wait_send()
    back_near.wait_send()
    pair_copy.wait_send()
    agf_first.wait_send()

    @pl.loop(1, pairs)
    def _(k):
        hist_copy(k).wait_send()
        fwd_copy(k).wait_send()
        rs_copy(k).wait_send()
        ag_copy(k).wait_send()
        agf_copy(k).wait_send()


def hand_over(count, *refs):
    given, taken, held = refs[:count], refs[count : 2 * count], refs[2 * count : 3 * count]
    sems = refs[-1]
    into = [pltpu.make_async_copy(given[i], held[i], sems.at[0, i]) for i in range(count)]
    out = [pltpu.make_async_copy(held[i], taken[i], sems.at[1, i]) for i in range(count)]
    for copy in into:
        copy.start()
    for i in range(count):
        into[i].wait()
        out[i].start()
    for copy in out:
        copy.wait()


def body(
    node_feats,
    tile_vals,
    tile_cols,
    tile_count,
    hist_cache,
    bound_ids,
    bound_wts,
    w_self,
    w_neigh,
    out_bias,
    out_grad,
):
    row_blocks, slots, tile, _ = tile_vals.shape
    rows, feat = node_feats.shape
    count = lax.axis_size("dom")
    pairs = count // 2
    hist = count * hist_cache.shape[0]
    chunk = 2 * feat * feat // (128 * count)

    vmem = pl.BlockSpec(memory_space=pltpu.VMEM)
    anywhere = pl.BlockSpec(memory_space=pl.ANY)
    dma = pltpu.SemaphoreType.DMA
    outs = pl.pallas_call(
        functools.partial(layer_kernel, count),
        out_shape=(
            jax.ShapeDtypeStruct((rows, feat), BF16),
            jax.ShapeDtypeStruct((rows, feat), BF16),
            jax.ShapeDtypeStruct((feat, feat), F32),
            jax.ShapeDtypeStruct((feat, feat), F32),
            jax.ShapeDtypeStruct((2, feat // 2), F32),
        ),
        in_specs=[pl.BlockSpec(memory_space=pltpu.SMEM)] + [vmem] * 3 + [anywhere] * 7,
        out_specs=(vmem,) * 5,
        scratch_shapes=[
            pltpu.VMEM(bound_wts.shape, BF16),
            pltpu.VMEM((feat, feat), BF16),
            pltpu.VMEM((feat, feat), BF16),
            pltpu.VMEM((rows, feat), BF16),
            pltpu.VMEM(tile_vals.shape, BF16),
            pltpu.VMEM((rows, 3 * rows + hist), BF16),
            pltpu.VMEM((3 * rows + hist, feat), BF16),
            pltpu.VMEM((rows, feat), F32),
            pltpu.VMEM((rows, feat), F32),
            pltpu.VMEM((rows, feat), F32),
            pltpu.VMEM((rows, feat), BF16),
            pltpu.VMEM((rows, feat), BF16),
            pltpu.VMEM((feat, rows), BF16),
            pltpu.VMEM((feat, rows), F32),
            pltpu.VMEM((feat, rows), BF16),
            pltpu.VMEM((feat, rows), BF16),
            pltpu.VMEM((feat, rows), BF16),
            pltpu.VMEM((feat, rows), BF16),
            pltpu.VMEM((2, pairs, chunk + 16, 128), BF16),
            pltpu.VMEM((pairs, chunk + 16, 128), BF16),
            pltpu.VMEM((pairs, chunk + 16, 128), BF16),
            pltpu.VMEM((pairs, chunk + 16, 128), BF16),
            pltpu.VMEM((count, chunk, 128), BF16),
            pltpu.VMEM((16, 128), F32),
            pltpu.VMEM((row_blocks, 128), jnp.int32),
            pltpu.SMEM((row_blocks, 128), jnp.int32),
            dma((8,)),
            dma((3,)),
            dma((3,)),
            dma((2,)),
            dma((2,)),
            dma((pairs,)),
            dma((pairs,)),
            dma((pairs,)),
            dma((pairs,)),
            dma((2,)),
            dma((pairs,)),
            dma((pairs,)),
            dma((pairs,)),
            dma((pairs,)),
            dma((pairs,)),
            dma((pairs,)),
        ],
        compiler_params=pltpu.CompilerParams(
            collective_id=0, has_side_effects=True, vmem_limit_bytes=56 * 1024 * 1024
        ),
    )(
        tile_count,
        tile_cols,
        bound_ids,
        out_bias.reshape(1, feat),
        bound_wts,
        w_self,
        w_neigh,
        out_grad,
        node_feats,
        hist_cache,
        tile_vals,
    )
    outs = pl.pallas_call(
        functools.partial(hand_over, 5),
        out_shape=tuple(jax.ShapeDtypeStruct(o.shape, o.dtype) for o in outs),
        in_specs=[anywhere] * 5,
        out_specs=(anywhere,) * 5,
        scratch_shapes=[pltpu.VMEM(o.shape, o.dtype) for o in outs] + [dma((2, 5))],
        compiler_params=pltpu.CompilerParams(vmem_limit_bytes=56 * 1024 * 1024),
    )(*outs)
    return outs[:4] + (outs[4].reshape(feat),)


def solution(mesh):
    placed = (
        P(("groups", "dom"), None),
        P(("groups", "dom"), None, None, None),
        P(("groups", "dom"), None),
        P(("groups", "dom")),
        P(("groups", "dom"), None),
        P(("groups", "dom"), None),
        P(("groups", "dom"), None),
        P(),
        P(),
        P(),
        P(("groups", "dom"), None),
    )
    return jax.shard_map(
        body,
        mesh=mesh,
        in_specs=placed,
        out_specs=(
            P(("groups", "dom"), None),
            P(("groups", "dom"), None),
            P("groups", None),
            P("groups", None),
            P("groups"),
        ),
        check_vma=False,
    )
```

```python
import functools
import math

import jax
import jax.numpy as jnp
from jax import lax
from jax.experimental import pallas as pl
from jax.experimental.pallas import tpu as pltpu
from jax.sharding import PartitionSpec as P

MESH = pl.DeviceIdType.MESH
F32 = jnp.float32
BF16 = jnp.bfloat16
NN = (((1,), (0,)), ((), ()))
NT = (((1,), (1,)), ((), ()))


def mm(a, b, dims):
    return lax.dot_general(a, b, dims, preferred_element_type=F32)


def layer_kernel(
    count,
    live_ref,
    cols_ref,
    ids_ref,
    bias_ref,
    wts_hbm,
    ws_hbm,
    wn_hbm,
    og_hbm,
    x_hbm,
    hist_hbm,
    tiles_hbm,
    hid_ref,
    feat_ref,
    gself_ref,
    gneigh_ref,
    gbias_ref,
    wts_ref,
    ws_ref,
    wn_ref,
    og_ref,
    tiles,
    band,
    ext,
    rdeg,
    base,
    pre_s,
    dz_s,
    x_t,
    agg_t,
    scaled_t,
    own_t,
    out_far,
    out_near,
    in_far,
    in_near,
    gsend,
    gpair,
    gsum,
    grecv,
    gfin,
    brow,
    code_vec,
    code_ref,
    local_sem,
    halo_send,
    halo_recv,
    back_send,
    back_recv,
    hist_send,
    hist_recv,
    fwd_send,
    fwd_recv,
    pair_sem,
    rs_send,
    rs_recv,
    ag_send,
    ag_recv,
    agf_send,
    agf_recv,
):
    rows = x_hbm.shape[0]
    feat = x_hbm.shape[1]
    row_blocks, slots, tile, _ = tiles.shape
    hrows = hist_hbm.shape[0]
    hist = count * hrows
    hbase = 3 * rows
    pairs = count // 2
    chunk = gfin.shape[1]
    inv_scale = 1.0 / math.sqrt(count * rows)
    step = 256
    half = rows // 2

    me = lax.axis_index("dom")
    side = lax.rem(me, 2)
    partner = me + 1 - 2 * side
    far = lax.rem(me + count - 1 + 2 * side, count)

    def peer_of(k):
        return lax.rem(me + 2 * k, count)

    def source_of(k):
        return lax.rem(me + count - 2 * k, count)

    def remote(src, dst, send, recv, peer):
        return pltpu.make_async_remote_copy(
            src_ref=src,
            dst_ref=dst,
            send_sem=send,
            recv_sem=recv,
            device_id={"dom": peer},
            device_id_type=MESH,
        )

    def greet(peer):
        pl.semaphore_signal(barrier, inc=1, device_id={"dom": peer}, device_id_type=MESH)

    barrier = pltpu.get_barrier_semaphore()
    greet(far)
    greet(partner)

    @pl.loop(1, pairs)
    def _(k):
        greet(peer_of(k))

    own_rows = pl.ds(pl.multiple_of(hbase + me * hrows, hrows), hrows)
    pieces = (
        (wts_hbm, wts_ref),
        (hist_hbm, ext.at[own_rows]),
        (x_hbm, ext.at[pl.ds(rows, rows)]),
        (ws_hbm, ws_ref),
        (wn_hbm, wn_ref),
        (tiles_hbm, tiles),
        (og_hbm, og_ref),
    )
    loads = [pltpu.make_async_copy(a, b, local_sem.at[i]) for i, (a, b) in enumerate(pieces)]
    for load in loads:
        load.start()

    pl.semaphore_wait(barrier, pairs + 1)

    far_there = (1 - side) * 2 * rows
    near_there = side * 2 * rows
    far_here = side * 2 * rows
    near_here = (1 - side) * 2 * rows

    def halo_far(j):
        at = pl.ds(pl.multiple_of(far_there + j * half, half), half)
        return remote(
            x_hbm.at[pl.ds(j * half, half)], ext.at[at], halo_send.at[j], halo_recv.at[j], far
        )

    halo_near = remote(
        x_hbm,
        ext.at[pl.ds(pl.multiple_of(near_there, rows), rows)],
        halo_send.at[2],
        halo_recv.at[2],
        partner,
    )

    quads = count // 4
    twin = me + 2 - 4 * lax.rem(me // 2, 2)

    def shard(i):
        return ext.at[pl.ds(pl.multiple_of(hbase + i * hrows, hrows), hrows)]

    def hop(owner, k, slot):
        return remote(
            shard(owner), shard(owner), hist_send.at[slot], hist_recv.at[slot], peer_of(2 * k)
        )

    def fwd_copy(slot):
        second = slot // quads
        src = source_of(2 * lax.rem(slot, quads))
        src = src + second * (2 - 4 * lax.rem(me // 2, 2))
        return remote(shard(src), shard(src), fwd_send.at[slot], fwd_recv.at[slot], partner)

    to_twin = remote(shard(me), shard(me), hist_send.at[0], hist_recv.at[0], twin)
    loads[1].wait()
    to_twin.start()

    @pl.loop(1, quads)
    def _(k):
        hop(me, k, k).start()

    halo_far(0).start()
    fwd_copy(0).start()
    halo_near.start()

    blocks = count * row_blocks
    pos = cols_ref[...] - (me - 1) * row_blocks
    pos = jnp.where(pos < 0, pos + blocks, jnp.where(pos >= blocks, pos - blocks, pos))
    block_of = lax.broadcasted_iota(jnp.int32, code_vec.shape, 0)
    place = lax.broadcasted_iota(jnp.int32, code_vec.shape, 1)
    limit = jnp.zeros(code_vec.shape, jnp.int32)
    for b in range(row_blocks):
        limit = jnp.where(block_of == b, live_ref[b], limit)
    code = jnp.full(code_vec.shape, -1, jnp.int32)
    for s in range(slots):
        code = jnp.where((pos[:, s : s + 1] == place) & (limit > s), s, code)
    code_vec[...] = code
    code_copy = pltpu.make_async_copy(code_vec, code_ref, local_sem.at[len(pieces)])
    code_copy.start()

    hstep = min(hist, 512)
    loads[0].wait()

    @pl.loop(0, row_blocks)
    def _(b):
        at = pl.ds(pl.multiple_of(b * tile, tile), tile)
        ids = ids_ref[pl.ds(b, 1), :]
        wts = wts_ref[at, :]
        for h in range(0, hist, hstep):
            hot = lax.broadcasted_iota(jnp.int32, (hstep, tile), 0) + h == ids
            hot = jnp.where(hot, 1.0, 0.0).astype(BF16)
            band[at, hbase + h : hbase + h + hstep] = mm(wts, hot, NT).astype(BF16)

    to_twin.wait_recv()

    @pl.loop(1, quads)
    def _(k):
        hop(twin, k, quads + k).start()

    halo_far(1).start()
    fwd_copy(quads).start()
    loads[0:2] = []
    for load in loads:
        load.wait()
    code_copy.wait()

    @pl.loop(0, row_blocks)
    def _(b):
        at = pl.ds(pl.multiple_of(b * tile, tile), tile)
        total = wts_ref[at, :].astype(F32)
        for p in range(slots):
            code = code_ref[b, p]
            live = jnp.where(code >= 0, 1.0, 0.0)
            part = tiles[b, jnp.maximum(code, 0)].astype(F32) * live
            total = total + part
            band[at, p * tile : (p + 1) * tile] = part.astype(BF16)
        degree = 1.0 + jnp.sum(total, axis=1, keepdims=True)
        rdeg[at, :] = jnp.broadcast_to(1.0 / degree, (tile, feat))

    @pl.loop(1, quads)
    def _(k):
        hop(me, k, k).wait_recv()
        fwd_copy(k).start()

    @pl.loop(1, quads)
    def _(k):
        hop(twin, k, quads + k).wait_recv()
        fwd_copy(quads + k).start()

    @pl.loop(0, rows // step)
    def _(r):
        at = pl.ds(pl.multiple_of(r * step, step), step)
        own = ext[pl.ds(pl.multiple_of(rows + r * step, step), step), :]
        base[at, :] = mm(band[at, rows : 2 * rows], ext[rows : 2 * rows, :], NN)
        x_t[:, at] = own.T
        pre_s[at, :] = mm(own, ws_ref[...], NN) + bias_ref[...]

    near_at = pl.ds(pl.multiple_of(near_here, rows), rows)
    far_half = [pl.ds(pl.multiple_of(far_here + j * half, half), half) for j in range(2)]
    halo_near.wait_recv()
    halo_far(0).wait_recv()

    @pl.loop(0, rows // step)
    def _(r):
        at = pl.ds(pl.multiple_of(r * step, step), step)
        base[at, :] += mm(band[at, near_at], ext[near_at, :], NN) + mm(
            band[at, far_half[0]], ext[far_half[0], :], NN
        )

    @pl.loop(0, pairs)
    def _(k):
        fwd_copy(k).wait_recv()

    @pl.loop(0, rows // step)
    def _(r):
        at = pl.ds(pl.multiple_of(r * step, step), step)
        base[at, :] += mm(band[at, hbase:], ext[hbase:, :], NN)

    halo_far(1).wait_recv()

    for r in range(rows // step):
        at = pl.ds(r * step, step)
        num = base[at, :] + mm(band[at, far_half[1]], ext[far_half[1], :], NN)
        recip = rdeg[at, :]
        agg = (num * recip).astype(BF16)
        pre = pre_s[at, :] + mm(agg, wn_ref[...], NN)
        sig = jax.nn.sigmoid(pre)
        hid_ref[at, :] = (pre * sig).astype(BF16)
        dz = (og_ref[at, :].astype(F32) * sig * (1.0 + pre * (1.0 - sig))).astype(BF16)
        scaled = (mm(dz, wn_ref[...], NT) * recip).astype(BF16)
        dz_s[at, :] = dz
        scaled_t[:, at] = scaled.T
        agg_t[:, at] = agg.T

    def back_far(j):
        return remote(out_far.at[j], in_far.at[j], back_send.at[j], back_recv.at[j], far)

    back_near = remote(out_near, in_near, back_send.at[2], back_recv.at[2], partner)
    dz = dz_s[...]
    bias_sum = jnp.sum(dz.astype(F32), axis=0, keepdims=True)
    row = lax.broadcasted_iota(jnp.int32, (16, 128), 0)
    bias_rows = jnp.where(
        row == 0, bias_sum[:, :128], jnp.where(row == 1, bias_sum[:, 128:], 0.0)
    ).astype(BF16)
    grads = (mm(x_t[...], dz, NN), mm(agg_t[...], dz, NN))
    for j in range(count):
        quarter, start = divmod(j * chunk, feat)
        lanes = (quarter % 2) * 128
        part = grads[quarter // 2][start : start + chunk, lanes : lanes + 128]
        gsend[j % 2, j // 2, :chunk, :] = part.astype(BF16)
        gsend[j % 2, j // 2, chunk:, :] = bias_rows

    pair_copy = remote(gsend.at[1 - side], gpair, pair_sem.at[0], pair_sem.at[1], partner)
    pair_copy.start()

    for j in range(2):
        out_far[j] = mm(scaled_t[...], band[:, far_half[j]], NN).astype(BF16)

    chip = me // 2

    def rs_copy(k):
        peer = peer_of(k)
        return remote(
            gsum.at[peer // 2], grecv.at[chip], rs_send.at[k], rs_recv.at[k], peer
        )

    def ag_copy(k):
        return remote(gfin.at[me], gfin.at[me], ag_send.at[k], ag_recv.at[k], peer_of(k))

    def agf_copy(k):
        src = source_of(k)
        return remote(gfin.at[src], gfin.at[src], agf_send.at[k], agf_recv.at[k], partner)

    pair_copy.wait_recv()
    gsum[...] = (gsend[side].astype(F32) + gpair[...].astype(F32)).astype(BF16)

    @pl.loop(1, pairs)
    def _(k):
        rs_copy(k).start()

    back_far(0).start()

    out_near[...] = mm(scaled_t[...], band[:, near_at], NN).astype(BF16)
    back_near.start()
    own_t[...] = mm(scaled_t[...], band[:, rows : 2 * rows], NN) + mm(ws_ref[...], dz, NT)

    @pl.loop(1, pairs)
    def _(k):
        rs_copy(k).wait_recv()

    def add(k, total):
        return total + grecv[lax.rem(chip + k, pairs)].astype(F32)

    total = lax.fori_loop(1, pairs, add, gsum[chip].astype(F32))
    gfin[me] = (total[:chunk] * inv_scale).astype(BF16)
    agf_first = agf_copy(0)
    agf_first.start()

    @pl.loop(1, pairs)
    def _(k):
        ag_copy(k).start()

    back_far(1).start()

    brow[...] = total[chunk:] * inv_scale
    gbias_ref[...] = brow[0:2, :]

    @pl.loop(1, pairs)
    def _(k):
        ag_copy(k).wait_recv()
        agf_copy(k).start()

    back_near.wait_recv()
    for j in range(2):
        back_far(j).wait_recv()
        for r in range(half // step):
            at = pl.ds(j * half + r * step, step)
            late = in_far[j, :, r * step : (r + 1) * step].astype(F32)
            spread = own_t[:, at] + in_near[:, at].astype(F32) + late
            feat_ref[at, :] = spread.astype(BF16).T

    agf_first.wait_recv()

    @pl.loop(1, pairs)
    def _(k):
        agf_copy(k).wait_recv()

    for j in range(count):
        quarter, start = divmod(j * chunk, feat)
        lanes = (quarter % 2) * 128
        out = gself_ref if quarter < 2 else gneigh_ref
        out[start : start + chunk, lanes : lanes + 128] = gfin[j].astype(F32)

    to_twin.wait_send()
    halo_far(0).wait_send()
    halo_far(1).wait_send()
    halo_near.wait_send()
    back_far(0).wait_send()
    back_far(1).wait_send()
    back_near.wait_send()
    pair_copy.wait_send()
    agf_first.wait_send()

    @pl.loop(1, quads)
    def _(k):
        hop(me, k, k).wait_send()
        hop(twin, k, quads + k).wait_send()

    @pl.loop(0, pairs)
    def _(k):
        fwd_copy(k).wait_send()

    @pl.loop(1, pairs)
    def _(k):
        rs_copy(k).wait_send()
        ag_copy(k).wait_send()
        agf_copy(k).wait_send()


def hand_over(count, *refs):
    given, taken, held = refs[:count], refs[count : 2 * count], refs[2 * count : 3 * count]
    sems = refs[-1]
    into = [pltpu.make_async_copy(given[i], held[i], sems.at[0, i]) for i in range(count)]
    out = [pltpu.make_async_copy(held[i], taken[i], sems.at[1, i]) for i in range(count)]
    for copy in into:
        copy.start()
    for i in range(count):
        into[i].wait()
        out[i].start()
    for copy in out:
        copy.wait()


def body(
    node_feats,
    tile_vals,
    tile_cols,
    tile_count,
    hist_cache,
    bound_ids,
    bound_wts,
    w_self,
    w_neigh,
    out_bias,
    out_grad,
):
    row_blocks, slots, tile, _ = tile_vals.shape
    rows, feat = node_feats.shape
    count = lax.axis_size("dom")
    pairs = count // 2
    hist = count * hist_cache.shape[0]
    chunk = 2 * feat * feat // (128 * count)

    vmem = pl.BlockSpec(memory_space=pltpu.VMEM)
    anywhere = pl.BlockSpec(memory_space=pl.ANY)
    dma = pltpu.SemaphoreType.DMA
    outs = pl.pallas_call(
        functools.partial(layer_kernel, count),
        out_shape=(
            jax.ShapeDtypeStruct((rows, feat), BF16),
            jax.ShapeDtypeStruct((rows, feat), BF16),
            jax.ShapeDtypeStruct((feat, feat), F32),
            jax.ShapeDtypeStruct((feat, feat), F32),
            jax.ShapeDtypeStruct((2, feat // 2), F32),
        ),
        in_specs=[pl.BlockSpec(memory_space=pltpu.SMEM)] + [vmem] * 3 + [anywhere] * 7,
        out_specs=(vmem,) * 5,
        scratch_shapes=[
            pltpu.VMEM(bound_wts.shape, BF16),
            pltpu.VMEM((feat, feat), BF16),
            pltpu.VMEM((feat, feat), BF16),
            pltpu.VMEM((rows, feat), BF16),
            pltpu.VMEM(tile_vals.shape, BF16),
            pltpu.VMEM((rows, 3 * rows + hist), BF16),
            pltpu.VMEM((3 * rows + hist, feat), BF16),
            pltpu.VMEM((rows, feat), F32),
            pltpu.VMEM((rows, feat), F32),
            pltpu.VMEM((rows, feat), F32),
            pltpu.VMEM((rows, feat), BF16),
            pltpu.VMEM((feat, rows), BF16),
            pltpu.VMEM((feat, rows), BF16),
            pltpu.VMEM((feat, rows), BF16),
            pltpu.VMEM((feat, rows), F32),
            pltpu.VMEM((2, feat, rows // 2), BF16),
            pltpu.VMEM((feat, rows), BF16),
            pltpu.VMEM((2, feat, rows // 2), BF16),
            pltpu.VMEM((feat, rows), BF16),
            pltpu.VMEM((2, pairs, chunk + 16, 128), BF16),
            pltpu.VMEM((pairs, chunk + 16, 128), BF16),
            pltpu.VMEM((pairs, chunk + 16, 128), BF16),
            pltpu.VMEM((pairs, chunk + 16, 128), BF16),
            pltpu.VMEM((count, chunk, 128), BF16),
            pltpu.VMEM((16, 128), F32),
            pltpu.VMEM((row_blocks, 128), jnp.int32),
            pltpu.SMEM((row_blocks, 128), jnp.int32),
            dma((8,)),
            dma((3,)),
            dma((3,)),
            dma((3,)),
            dma((3,)),
            dma((pairs,)),
            dma((pairs,)),
            dma((pairs,)),
            dma((pairs,)),
            dma((2,)),
            dma((pairs,)),
            dma((pairs,)),
            dma((pairs,)),
            dma((pairs,)),
            dma((pairs,)),
            dma((pairs,)),
        ],
        compiler_params=pltpu.CompilerParams(
            collective_id=0, has_side_effects=True, vmem_limit_bytes=56 * 1024 * 1024
        ),
    )(
        tile_count,
        tile_cols,
        bound_ids,
        out_bias.reshape(1, feat),
        bound_wts,
        w_self,
        w_neigh,
        out_grad,
        node_feats,
        hist_cache,
        tile_vals,
    )
    outs = pl.pallas_call(
        functools.partial(hand_over, 5),
        out_shape=tuple(jax.ShapeDtypeStruct(o.shape, o.dtype) for o in outs),
        in_specs=[anywhere] * 5,
        out_specs=(anywhere,) * 5,
        scratch_shapes=[pltpu.VMEM(o.shape, o.dtype) for o in outs] + [dma((2, 5))],
        compiler_params=pltpu.CompilerParams(vmem_limit_bytes=56 * 1024 * 1024),
    )(*outs)
    return outs[:4] + (outs[4].reshape(feat),)


def solution(mesh):
    placed = (
        P(("groups", "dom"), None),
        P(("groups", "dom"), None, None, None),
        P(("groups", "dom"), None),
        P(("groups", "dom")),
        P(("groups", "dom"), None),
        P(("groups", "dom"), None),
        P(("groups", "dom"), None),
        P(),
        P(),
        P(),
        P(("groups", "dom"), None),
    )
    return jax.shard_map(
        body,
        mesh=mesh,
        in_specs=placed,
        out_specs=(
            P(("groups", "dom"), None),
            P(("groups", "dom"), None),
            P("groups", None),
            P("groups", None),
            P("groups"),
        ),
        check_vma=False,
    )
```
